32 devices in a mesh: req: 16 (over z, y, core), tp: 2 (over x).
Axes of the slice: x: 2, y: 2, z: 4, core: 2. Of those that a mesh axis runs over, the one named last changes fastest.
Arguments:
- tokens: bfloat16 [8192, 1024], P(('req', 'tp')), may hold values from -6 to 6
- w_qkv: bfloat16 [1024, 3, 1024], P(None, None, 'tp'), may hold values from -0.1875 to 0.1875
- w_out: bfloat16 [1024, 1024], P('tp'), may hold values from -0.75 to 0.75
- w_up: bfloat16 [1024, 4096], P(None, 'tp'), may hold values from -0.1875 to 0.1875
- b_up: float32 [4096], P('tp'), may hold values from -4 to 4
- w_down: bfloat16 [4096, 1024], P('tp'), may hold values from -0.09375 to 0.09375
- b_down: float32 [1024], replicated, may hold values from -3 to 3
- ln1_gain: float32 [1024], replicated, may hold values from 0.5 to 1.5
- ln1_bias: float32 [1024], replicated, may hold values from -3 to 3
- ln2_gain: float32 [1024], replicated, may hold values from 0.5 to 1.5
- ln2_bias: float32 [1024], replicated, may hold values from -3 to 3
- kv_cache: bfloat16 [2, 16, 16384, 1024], P(None, None, 'req', 'tp'), may hold values from -122 to 122
- cache_len: int32 [16], replicated, may hold values from 0 to 16384, as said below
- span_len: int32 [16], replicated, may hold values from 1 to 512, as said below
Outputs:
- output: bfloat16 [8192, 1024], P(('req', 'tp'))
The draws below stay inside these ranges and needn't reach their ends.
Inputs may be any that keep to these rules, and one draw needn't show every extreme that they name: The first cache_len[r] positions of request r hold its keys and values; some request has 16384. Slots from span_len[r] on are padding whose keys are not attended to; some request has 512.
All inputs are finite; a program needn't handle non-finite values.
Results may differ from the reference program's by a relative error of at most 0.015.
Values may be sent and summed in bfloat16 or wider, within the bound.
A program may use at most 256 MiB of HBM per device.

```python
import jax
import jax.numpy as jnp
from jax import lax

D = 1024
HEADS = 16
HEAD_DIM = 64
FF = 4096
SPAN = 512
CAP = 16384
REQUESTS = 16
TOKENS = 8192
BLOCK = 1024
N_REQ = 16


def draw_kv_cache(key, part):
    full_shape = (2, REQUESTS, CAP, D)
    first = jax.random.fold_in(jax.random.fold_in(key, 11), 0)
    result = 2.0 * jax.random.normal(first, full_shape, jnp.float32)
    return result.astype(jnp.bfloat16)


def draw_cache_len(key, part):
    first, second, third = jax.random.split(jax.random.fold_in(key, 23), 3)
    background = jax.random.randint(first, (REQUESTS,), 0, CAP + 1)
    shifts = jax.random.randint(second, (REQUESTS,), 0, 3)
    lengths = background // jnp.left_shift(jnp.ones_like(shifts), shifts)
    longest = jax.random.randint(third, (), 0, REQUESTS)
    return jnp.where(jnp.arange(REQUESTS) == longest, CAP, lengths).astype(jnp.int32)


def draw_span_len(key, part):
    first, second = jax.random.split(jax.random.fold_in(key, 37), 2)
    lengths = jax.random.randint(first, (REQUESTS,), 1, SPAN + 1)
    longest = jax.random.randint(second, (), 0, REQUESTS)
    return jnp.where(jnp.arange(REQUESTS) == longest, SPAN, lengths).astype(jnp.int32)


def block_scale(stream_key, shape, cuts, smallest, largest):
    level, own = 1.0, jax.random.fold_in(stream_key, 6)
    for position, blocks in cuts:
        draws = jnp.exp(jax.random.uniform(jax.random.fold_in(own, position), (blocks,), jnp.float32, smallest / len(cuts), largest / len(cuts)))
        level = level * jnp.repeat(draws, shape[position] // blocks).reshape([-1 if axis == position else 1 for axis in range(len(shape))])
    return level


def noise(rng, shape, scale, reach, pieces=(), kind=jnp.bfloat16):
    values = scale * jax.random.normal(rng, shape, jnp.float32)
    if pieces:
        values = values * block_scale(rng, shape, pieces, -0.22, 0.18)
    return jnp.clip(values, -reach, reach).astype(kind)


def setup_inputs(seed: int = 0) -> dict:
    streams_of = jax.random.split(jax.random.key(seed), 15)
    tokens = noise(streams_of[0], (TOKENS, D), 1.0, 6.0, ((0, 32),))
    w_qkv = noise(streams_of[1], (D, 3, D), D ** -0.5, 0.1875, ((2, 2),))
    w_out = noise(streams_of[2], (D, D), HEAD_DIM ** -0.5, 0.75, ((0, 2),))
    w_up = noise(streams_of[3], (D, FF), D ** -0.5, 0.1875, ((1, 2),))
    b_up = noise(streams_of[4], (FF,), 1.0, 4.0, ((0, 2),), jnp.float32)
    w_down = noise(streams_of[5], (FF, D), FF ** -0.5, 0.09375, ((0, 2),))
    b_down = noise(streams_of[6], (D,), 0.5, 3.0, (), jnp.float32)
    ln1_gain = jnp.clip(1.0 + 0.1 * jax.random.normal(streams_of[7], (D,), jnp.float32), 0.5, 1.5)
    ln1_bias = noise(streams_of[8], (D,), 0.5, 3.0, (), jnp.float32)
    ln2_gain = jnp.clip(1.0 + 0.1 * jax.random.normal(streams_of[9], (D,), jnp.float32), 0.5, 1.5)
    ln2_bias = noise(streams_of[10], (D,), 0.5, 3.0, (), jnp.float32)
    kv_cache = draw_kv_cache(jax.random.fold_in(streams_of[14], 71), 0)
    cache_len = draw_cache_len(jax.random.fold_in(streams_of[14], 71), 0)
    span_len = draw_span_len(jax.random.fold_in(streams_of[14], 71), 0)
    return dict(tokens=tokens, w_qkv=w_qkv, w_out=w_out, w_up=w_up, b_up=b_up, w_down=w_down, b_down=b_down, ln1_gain=ln1_gain, ln1_bias=ln1_bias, ln2_gain=ln2_gain, ln2_bias=ln2_bias, kv_cache=kv_cache, cache_len=cache_len, span_len=span_len)


masked_score = -1e+30

def layer_norm(values, gain, bias):
    centre = lax.optimization_barrier(jnp.mean(values, axis=-1, keepdims=True))
    centred = values - centre
    variance = lax.optimization_barrier(jnp.mean(centred * centred, axis=-1, keepdims=True))
    return centred * lax.rsqrt(variance + 1e-05) * gain + bias

def partial_attention(queries, key_rows, value_rows, allowed):
    scores = jnp.einsum('chd,nhd->hcn', queries.astype(jnp.float32), key_rows.astype(jnp.float32)) * queries.shape[-1] ** (-0.5)
    scores = jnp.where(allowed[None], scores, masked_score)
    peaks = lax.optimization_barrier(jnp.max(scores, axis=-1))
    weights = jnp.where(allowed[None], jnp.exp(scores - peaks[..., None]), 0.0).astype(jnp.bfloat16)
    weight_sums = lax.optimization_barrier(jnp.sum(weights.astype(jnp.float32), axis=-1))
    blended = jnp.einsum('hcn,nhd->chd', weights.astype(jnp.float32), value_rows.astype(jnp.float32))
    return (peaks.T, weight_sums.T, blended.reshape(blended.shape[0], -1))

def merge_axis(peaks, weight_sums, blended, axis):
    highest = lax.optimization_barrier(jnp.max(peaks, axis=axis, keepdims=True))
    factors = jnp.exp(peaks - highest)
    sums_out = lax.optimization_barrier(jnp.sum(factors * weight_sums, axis=axis))
    spread = jnp.repeat(factors, blended.shape[-1] // peaks.shape[-1], axis=-1)
    blend_out = lax.optimization_barrier(jnp.sum(spread * blended, axis=axis))
    return (jnp.squeeze(highest, axis=axis), sums_out, blend_out)

def reference(tokens, w_qkv, w_out, w_up, b_up, w_down, b_down, ln1_gain, ln1_bias, ln2_gain, ln2_bias, kv_cache, cache_len, span_len):
    heads_qkv = jnp.dot(tokens, w_qkv.reshape(D, 3 * D), preferred_element_type=jnp.float32).astype(jnp.bfloat16)
    four_shape = (REQUESTS, SPAN, HEADS, HEAD_DIM)
    queries = heads_qkv[:, :D].reshape(four_shape)
    fresh_keys = heads_qkv[:, D:2 * D].reshape(four_shape)
    fresh_values = heads_qkv[:, 2 * D:].reshape(four_shape)
    cached = kv_cache.reshape(2, REQUESTS, N_REQ, BLOCK, HEADS, HEAD_DIM)
    positions = jnp.arange(SPAN, dtype=jnp.int32)
    block_starts = jnp.arange(N_REQ, dtype=jnp.int32) * BLOCK

    def per_request(items):
        own_queries, own_keys, own_values, cache_keys, cache_values, cached_count, fresh_count = items
        allowed = (positions[None, :] <= positions[:, None]) & (positions[None, :] < fresh_count)
        fresh = partial_attention(own_queries, own_keys, own_values, allowed)

        def per_block(block):
            block_keys, block_values, start_pos = block
            places = start_pos + jnp.arange(BLOCK, dtype=jnp.int32)
            block_allowed = jnp.broadcast_to((places < cached_count)[None, :], (SPAN, BLOCK))
            return partial_attention(own_queries, block_keys, block_values, block_allowed)
        blocks = lax.map(per_block, (cache_keys, cache_values, block_starts))
        joined = [jnp.concatenate([fresh[index][None], blocks[index]], axis=0) for index in range(3)]
        peaks, weight_sums, blended = merge_axis(joined[0], joined[1], joined[2], 0)
        return (blended / jnp.repeat(weight_sums, HEAD_DIM, axis=-1)).astype(jnp.bfloat16)
    attention = lax.map(per_request, (queries, fresh_keys, fresh_values, cached[0], cached[1], cache_len, span_len))
    attention = attention.reshape(TOKENS, D)
    projected = jnp.dot(attention, w_out, preferred_element_type=jnp.float32)
    normed = layer_norm(tokens.astype(jnp.float32) + projected, ln1_gain, ln1_bias).astype(jnp.bfloat16)
    hidden = jax.nn.gelu(jnp.dot(normed, w_up, preferred_element_type=jnp.float32) + b_up, approximate=False).astype(jnp.bfloat16)
    summed = jnp.dot(hidden, w_down, preferred_element_type=jnp.float32) + b_down + normed.astype(jnp.float32)
    return layer_norm(summed, ln2_gain, ln2_bias).astype(jnp.bfloat16)
```

```python
import functools

import jax
import jax.numpy as jnp
from jax import lax
from jax.experimental import pallas as pl
from jax.experimental.pallas import tpu as pltpu
from jax.sharding import PartitionSpec as P

HEAD_DIM = 64
PAIR = 2 * HEAD_DIM
NEG = -1e30
ONES = 16
MESH = pl.DeviceIdType.MESH


def layer_norm(values, gain, bias):
    centre = jnp.mean(values, axis=-1, keepdims=True)
    centred = values - centre
    variance = jnp.mean(centred * centred, axis=-1, keepdims=True)
    return centred * lax.rsqrt(variance + 1e-05) * gain + bias


def ring_place(index, n):
    z, y, core = index // 4, (index // 2) % 2, index % 2
    chip = z + y * (n // 2 - 1 - 2 * z)
    return 2 * chip + core


def ring_index(place, n):
    chip, core = place // 2, place % 2
    y = chip // (n // 4)
    z = chip + y * (n // 2 - 1 - 2 * chip)
    return 4 * z + 2 * y + core


def attend(scores, v_t):
    peak = jnp.max(scores, axis=0, keepdims=True)
    weights = jnp.exp(scores - peak).astype(jnp.bfloat16)
    ones = jnp.ones((ONES, v_t.shape[1]), jnp.bfloat16)
    both = jnp.dot(
        jnp.concatenate([v_t, ones], axis=0), weights, preferred_element_type=jnp.float32
    )
    return peak, both[HEAD_DIM : HEAD_DIM + 1], both[:HEAD_DIM]


def ring_kernel(
    n,
    streams,
    len_ref,
    span_ref,
    q_ref,
    fk_ref,
    fv_ref,
    kv_ref,
    out_ref,
    q_buf,
    acc_buf,
    st_buf,
    kv_buf,
    bias_buf,
    loc_acc,
    loc_st,
    q_send,
    q_recv,
    a_send,
    a_recv,
    s_send,
    s_recv,
    kv_sem,
):
    width, slots = q_ref.shape
    keys = kv_buf.shape[3]
    lanes = width // streams
    heads = lanes // HEAD_DIM
    me = lax.axis_index("req")
    place = ring_place(me, n)
    right = ring_index((place + 1) % n, n)
    left = ring_index((place + n - 1) % n, n)
    onward = (right, left)

    barrier = pltpu.get_barrier_semaphore()
    for neighbour in (left, right):
        pl.semaphore_signal(barrier, inc=1, device_id={"req": neighbour}, device_id_type=MESH)

    def owner(j, s):
        return ring_index((place + n - s) % n if j == 0 else (place + s) % n, n)

    def rows(j):
        return pl.ds(j * lanes, lanes)

    def kv_copy(j, s):
        return pltpu.make_async_copy(
            kv_ref.at[:, owner(j, s), :, rows(j)], kv_buf.at[s % 2, j], kv_sem.at[s % 2, j]
        )

    def remote(src, dst, send, recv, j):
        return pltpu.make_async_remote_copy(
            src_ref=src,
            dst_ref=dst,
            send_sem=send,
            recv_sem=recv,
            device_id={"req": onward[j]},
            device_id_type=MESH,
        )

    def q_copy(j, s):
        return remote(
            q_buf.at[s, rows(j)], q_buf.at[s + 1, rows(j)], q_send.at[j, s], q_recv.at[j, s], j
        )

    def acc_copies(j, s):
        return (
            remote(
                acc_buf.at[s, rows(j)],
                acc_buf.at[s + 1, rows(j)],
                a_send.at[j, s],
                a_recv.at[j, s],
                j,
            ),
            remote(st_buf.at[s, j], st_buf.at[s + 1, j], s_send.at[j, s], s_recv.at[j, s], j),
        )

    for j in range(streams):
        kv_copy(j, 0).start()
    q_buf[0] = q_ref[...]
    pl.semaphore_wait(barrier, 2)

    lane = lax.broadcasted_iota(jnp.int32, (1, PAIR), 1)
    row = lax.broadcasted_iota(jnp.int32, (PAIR, 1), 0)
    keep = []
    spare = []
    for h in range(2):
        spare_at = HEAD_DIM * (1 - h)
        keep.append(jnp.where(lane == spare_at, 0.0, 1.0).astype(jnp.bfloat16))
        spare.append(spare_at)

    def masked_query(q_pair, h):
        own = q_pair[h * HEAD_DIM : (h + 1) * HEAD_DIM]
        first = lax.broadcasted_iota(jnp.int32, (HEAD_DIM, slots), 0) == 0
        other = jnp.where(first, 1.0, 0.0).astype(jnp.bfloat16)
        return jnp.concatenate([own, other] if h == 0 else [other, own], axis=0)

    def merged(j, slot, h):
        at = pl.ds(j * lanes + h * HEAD_DIM, HEAD_DIM)
        peak_a = st_buf[slot, j, h : h + 1, :]
        sum_a = st_buf[slot, j, heads + h : heads + h + 1, :]
        peak_b = loc_st[j, h : h + 1, :]
        sum_b = loc_st[j, heads + h : heads + h + 1, :]
        peak = jnp.maximum(peak_a, peak_b)
        fa = jnp.exp(peak_a - peak)
        fb = jnp.exp(peak_b - peak)
        blend = fa * acc_buf[slot, at, :].astype(jnp.float32) + fb * loc_acc[at, :]
        return at, peak, fa * sum_a + fb * sum_b, blend

    def step(s, carry):
        for j in range(streams):

            @pl.when(s + 1 < n)
            def _():
                kv_copy(j, s + 1).start()

            @pl.when(s > 0)
            def _():
                q_copy(j, s - 1).wait_recv()

            @pl.when(s + 1 < n)
            def _():
                q_copy(j, s).start()

        for j in range(streams):
            kv_copy(j, s).wait()
            limit = len_ref[owner(j, s)]
            position = me * keys + lax.broadcasted_iota(jnp.int32, (keys, PAIR), 0)
            lane_full = lax.broadcasted_iota(jnp.int32, (keys, PAIR), 1)
            for h in range(2):
                out = (position >= limit) & (lane_full == spare[h])
                bias_buf[h] = jnp.where(out, NEG, 0.0).astype(jnp.bfloat16)
            for g in range(lanes // PAIR):
                k_pair = kv_buf[s % 2, j, 0, :, g * PAIR : (g + 1) * PAIR]
                v_t = kv_buf[s % 2, j, 1, :, g * PAIR : (g + 1) * PAIR].T
                q_pair = q_buf[s, pl.ds(j * lanes + g * PAIR, PAIR), :]
                for h in range(2):
                    scores = jnp.dot(
                        k_pair * keep[h] + bias_buf[h],
                        masked_query(q_pair, h),
                        preferred_element_type=jnp.float32,
                    )
                    peak, total, blend = attend(scores, v_t[h * HEAD_DIM : (h + 1) * HEAD_DIM])
                    i = 2 * g + h
                    loc_st[j, i : i + 1, :] = peak
                    loc_st[j, heads + i : heads + i + 1, :] = total
                    loc_acc[pl.ds(j * lanes + i * HEAD_DIM, HEAD_DIM), :] = blend

            @pl.when(s == 0)
            def _():
                st_buf[0, j] = loc_st[j]
                acc_buf[0, rows(j), :] = loc_acc[rows(j), :].astype(jnp.bfloat16)

            @pl.when(s > 0)
            def _():
                for copy in acc_copies(j, s - 1):
                    copy.wait_recv()
                for h in range(heads):
                    at, peak, total, blend = merged(j, s, h)
                    st_buf[s, j, h : h + 1, :] = peak
                    st_buf[s, j, heads + h : heads + h + 1, :] = total
                    acc_buf[s, at, :] = blend.astype(jnp.bfloat16)

            for copy in acc_copies(j, s):
                copy.start()
        return carry

    lax.fori_loop(0, n, step, 0)

    limit = span_ref[me]
    key_at = lax.broadcasted_iota(jnp.int32, (slots, slots), 0)
    slot_at = lax.broadcasted_iota(jnp.int32, (slots, slots), 1)
    allowed = (key_at <= slot_at) & (key_at < limit)
    for j in range(streams):
        for g in range(lanes // PAIR):
            base = j * lanes + g * PAIR
            k_pair = fk_ref[:, base : base + PAIR]
            v_t = fv_ref[:, base : base + PAIR].T
            q_pair = q_ref[base : base + PAIR, :]
            for h in range(2):
                scores = jnp.dot(
                    k_pair * keep[h], masked_query(q_pair, h), preferred_element_type=jnp.float32
                )
                scores = jnp.where(allowed, scores, NEG)
                peak, total, blend = attend(scores, v_t[h * HEAD_DIM : (h + 1) * HEAD_DIM])
                i = 2 * g + h
                loc_st[j, i : i + 1, :] = peak
                loc_st[j, heads + i : heads + i + 1, :] = total
                loc_acc[pl.ds(j * lanes + i * HEAD_DIM, HEAD_DIM), :] = blend
    for j in range(streams):
        for copy in acc_copies(j, n - 1):
            copy.wait_recv()
        for h in range(heads):
            at, _, total, blend = merged(j, n, h)
            out_ref[at, :] = (blend / total).astype(jnp.bfloat16)

    def drain(s, carry):
        for j in range(streams):

            @pl.when(s + 1 < n)
            def _():
                q_copy(j, s).wait_send()

            for copy in acc_copies(j, s):
                copy.wait_send()
        return carry

    lax.fori_loop(0, n, drain, 0)


def ring_attention(n, q_t, fresh_k, fresh_v, kv, cache_len, span_len):
    width, slots = q_t.shape
    keys = kv.shape[2]
    streams = 2 if width % (2 * PAIR) == 0 else 1
    lanes = width // streams
    stat_rows = -(-2 * (lanes // HEAD_DIM) // 8) * 8
    requests = kv.shape[1]
    vmem = pl.BlockSpec(memory_space=pltpu.VMEM)
    smem = pl.BlockSpec(memory_space=pltpu.SMEM)
    dma = pltpu.SemaphoreType.DMA
    return pl.pallas_call(
        functools.partial(ring_kernel, n, streams),
        out_shape=jax.ShapeDtypeStruct((width, slots), jnp.bfloat16),
        in_specs=[smem, smem, vmem, vmem, vmem, pl.BlockSpec(memory_space=pl.ANY)],
        out_specs=vmem,
        scratch_shapes=[
            pltpu.VMEM((n, width, slots), jnp.bfloat16),
            pltpu.VMEM((n + 1, width, slots), jnp.bfloat16),
            pltpu.VMEM((n + 1, streams, stat_rows, slots), jnp.float32),
            pltpu.VMEM((2, streams, 2, keys, lanes), jnp.bfloat16),
            pltpu.VMEM((2, keys, PAIR), jnp.bfloat16),
            pltpu.VMEM((width, slots), jnp.float32),
            pltpu.VMEM((streams, stat_rows, slots), jnp.float32),
            dma((streams, n)),
            dma((streams, n)),
            dma((streams, n)),
            dma((streams, n)),
            dma((streams, n)),
            dma((streams, n)),
            dma((2, streams)),
        ],
        compiler_params=pltpu.CompilerParams(
            collective_id=0, has_side_effects=True, vmem_limit_bytes=56 * 1024 * 1024
        ),
        cost_estimate=pl.CostEstimate(
            flops=4 * requests * width * slots * keys,
            bytes_accessed=2 * requests * keys * width * 2,
            transcendentals=requests * (width // HEAD_DIM) * slots * keys,
        ),
    )(cache_len, span_len, q_t, fresh_k, fresh_v, kv)


def shards(
    n,
    tokens,
    w_qkv,
    w_out,
    w_up,
    b_up,
    w_down,
    b_down,
    ln1_gain,
    ln1_bias,
    ln2_gain,
    ln2_bias,
    kv_cache,
    cache_len,
    span_len,
):
    rows = lax.all_gather(tokens, "tp", axis=0, tiled=True)
    q_t = lax.dot_general(
        w_qkv[:, 0], rows, (((0,), (1,)), ((), ())), preferred_element_type=jnp.float32
    ).astype(jnp.bfloat16) * jnp.bfloat16(HEAD_DIM**-0.5)
    fresh_k = jnp.dot(rows, w_qkv[:, 1], preferred_element_type=jnp.float32).astype(jnp.bfloat16)
    fresh_v = jnp.dot(rows, w_qkv[:, 2], preferred_element_type=jnp.float32).astype(jnp.bfloat16)
    attention = ring_attention(n, q_t, fresh_k, fresh_v, kv_cache, cache_len, span_len)
    projected = lax.psum_scatter(
        lax.dot_general(
            attention, w_out, (((0,), (0,)), ((), ())), preferred_element_type=jnp.float32
        ).astype(jnp.bfloat16),
        "tp",
        scatter_dimension=0,
        tiled=True,
    ).astype(jnp.float32)
    normed = layer_norm(tokens.astype(jnp.float32) + projected, ln1_gain, ln1_bias).astype(
        jnp.bfloat16
    )
    hidden = jax.nn.gelu(
        jnp.dot(
            lax.all_gather(normed, "tp", axis=0, tiled=True),
            w_up,
            preferred_element_type=jnp.float32,
        )
        + b_up,
        approximate=False,
    ).astype(jnp.bfloat16)
    summed = lax.psum_scatter(
        jnp.dot(hidden, w_down, preferred_element_type=jnp.float32).astype(jnp.bfloat16),
        "tp",
        scatter_dimension=0,
        tiled=True,
    ).astype(jnp.float32)
    return layer_norm(summed + b_down + normed.astype(jnp.float32), ln2_gain, ln2_bias).astype(
        jnp.bfloat16
    )


def solution(mesh):
    placed = (
        P(("req", "tp"), None),
        P(None, None, "tp"),
        P("tp", None),
        P(None, "tp"),
        P("tp"),
        P("tp", None),
        P(),
        P(),
        P(),
        P(),
        P(),
        P(None, None, "req", "tp"),
        P(),
        P(),
    )
    return jax.shard_map(
        functools.partial(shards, mesh.shape["req"]),
        mesh=mesh,
        in_specs=placed,
        out_specs=P(("req", "tp"), None),
        check_vma=False,
    )
```

```python
import functools

import jax
import jax.numpy as jnp
from jax import lax
from jax.experimental import pallas as pl
from jax.experimental.pallas import tpu as pltpu
from jax.sharding import PartitionSpec as P

HEAD_DIM = 64
PAIR = 2 * HEAD_DIM
NEG = -1e30
ONES = 16
MESH = pl.DeviceIdType.MESH


def layer_norm(values, gain, bias):
    centre = jnp.mean(values, axis=-1, keepdims=True)
    centred = values - centre
    variance = jnp.mean(centred * centred, axis=-1, keepdims=True)
    return centred * lax.rsqrt(variance + 1e-05) * gain + bias


def ring_place(index, n):
    z, y, core = index // 4, (index // 2) % 2, index % 2
    chip = z + y * (n // 2 - 1 - 2 * z)
    return 2 * chip + core


def ring_index(place, n):
    chip, core = place // 2, place % 2
    y = chip // (n // 4)
    z = chip + y * (n // 2 - 1 - 2 * chip)
    return 4 * z + 2 * y + core


def attend(scores, v_t):
    peak = jnp.max(scores, axis=0, keepdims=True)
    weights = jnp.exp((scores - peak).astype(jnp.bfloat16))
    ones = jnp.ones((ONES, v_t.shape[1]), jnp.bfloat16)
    both = jnp.dot(
        jnp.concatenate([v_t, ones], axis=0), weights, preferred_element_type=jnp.float32
    )
    return peak, both[HEAD_DIM : HEAD_DIM + 1], both[:HEAD_DIM]


def ring_kernel(
    n,
    streams,
    len_ref,
    span_ref,
    q_ref,
    fk_ref,
    fv_ref,
    kv_ref,
    out_ref,
    q_buf,
    acc_buf,
    st_buf,
    kv_buf,
    bias_buf,
    loc_acc,
    loc_st,
    q_send,
    q_recv,
    a_send,
    a_recv,
    s_send,
    s_recv,
    kv_sem,
):
    width, slots = q_ref.shape
    keys = kv_buf.shape[3]
    lanes = width // streams
    heads = lanes // HEAD_DIM
    me = lax.axis_index("req")
    place = ring_place(me, n)
    right = ring_index((place + 1) % n, n)
    left = ring_index((place + n - 1) % n, n)
    onward = (right, left)

    barrier = pltpu.get_barrier_semaphore()
    for neighbour in (left, right):
        pl.semaphore_signal(barrier, inc=1, device_id={"req": neighbour}, device_id_type=MESH)

    def owner(j, s):
        return ring_index((place + n - s) % n if j == 0 else (place + s) % n, n)

    def rows(j):
        return pl.ds(j * lanes, lanes)

    def kv_copy(j, s):
        return pltpu.make_async_copy(
            kv_ref.at[:, owner(j, s), :, rows(j)], kv_buf.at[s % 2, j], kv_sem.at[s % 2, j]
        )

    def remote(src, dst, send, recv, j):
        return pltpu.make_async_remote_copy(
            src_ref=src,
            dst_ref=dst,
            send_sem=send,
            recv_sem=recv,
            device_id={"req": onward[j]},
            device_id_type=MESH,
        )

    def q_copy(j, s):
        return remote(
            q_buf.at[s, rows(j)], q_buf.at[s + 1, rows(j)], q_send.at[j, s], q_recv.at[j, s], j
        )

    def acc_copies(j, s):
        return (
            remote(
                acc_buf.at[s, rows(j)],
                acc_buf.at[s + 1, rows(j)],
                a_send.at[j, s],
                a_recv.at[j, s],
                j,
            ),
            remote(st_buf.at[s, j], st_buf.at[s + 1, j], s_send.at[j, s], s_recv.at[j, s], j),
        )

    for j in range(streams):
        kv_copy(j, 0).start()
    q_buf[0] = q_ref[...]
    pl.semaphore_wait(barrier, 2)

    lane = lax.broadcasted_iota(jnp.int32, (1, PAIR), 1)
    row = lax.broadcasted_iota(jnp.int32, (PAIR, 1), 0)
    keep = []
    spare = []
    for h in range(2):
        spare_at = HEAD_DIM * (1 - h)
        keep.append(jnp.where(lane == spare_at, 0.0, 1.0).astype(jnp.bfloat16))
        spare.append(spare_at)

    def masked_query(q_pair, h):
        own = q_pair[h * HEAD_DIM : (h + 1) * HEAD_DIM]
        first = lax.broadcasted_iota(jnp.int32, (HEAD_DIM, slots), 0) == 0
        other = jnp.where(first, 1.0, 0.0).astype(jnp.bfloat16)
        return jnp.concatenate([own, other] if h == 0 else [other, own], axis=0)

    def merged(j, slot, h):
        at = pl.ds(j * lanes + h * HEAD_DIM, HEAD_DIM)
        peak_a = st_buf[slot, j, h : h + 1, :]
        sum_a = st_buf[slot, j, heads + h : heads + h + 1, :]
        peak_b = loc_st[j, h : h + 1, :]
        sum_b = loc_st[j, heads + h : heads + h + 1, :]
        peak = jnp.maximum(peak_a, peak_b)
        fa = jnp.exp(peak_a - peak)
        fb = jnp.exp(peak_b - peak)
        blend = fa * acc_buf[slot, at, :].astype(jnp.float32) + fb * loc_acc[at, :]
        return at, peak, fa * sum_a + fb * sum_b, blend

    def step(s, carry):
        for j in range(streams):

            @pl.when(s + 1 < n)
            def _():
                kv_copy(j, s + 1).start()

            @pl.when(s > 0)
            def _():
                q_copy(j, s - 1).wait_recv()

            @pl.when(s + 1 < n)
            def _():
                q_copy(j, s).start()

        for j in range(streams):
            kv_copy(j, s).wait()
            limit = len_ref[owner(j, s)]
            position = me * keys + lax.broadcasted_iota(jnp.int32, (keys, PAIR), 0)
            lane_full = lax.broadcasted_iota(jnp.int32, (keys, PAIR), 1)
            for h in range(2):
                out = (position >= limit) & (lane_full == spare[h])
                bias_buf[h] = jnp.where(out, NEG, 0.0).astype(jnp.bfloat16)
            def scores_of(i):
                g, h = i // 2, i % 2
                k_pair = kv_buf[s % 2, j, 0, :, g * PAIR : (g + 1) * PAIR]
                q_pair = q_buf[s, pl.ds(j * lanes + g * PAIR, PAIR), :]
                return jnp.dot(
                    k_pair * keep[h] + bias_buf[h],
                    masked_query(q_pair, h),
                    preferred_element_type=jnp.float32,
                )

            later = scores_of(0)
            v_t = None
            for i in range(heads):
                scores = later
                if i + 1 < heads:
                    later = scores_of(i + 1)
                g, h = i // 2, i % 2
                if h == 0:
                    v_t = kv_buf[s % 2, j, 1, :, g * PAIR : (g + 1) * PAIR].T
                peak, total, blend = attend(scores, v_t[h * HEAD_DIM : (h + 1) * HEAD_DIM])
                loc_st[j, i : i + 1, :] = peak
                loc_st[j, heads + i : heads + i + 1, :] = total
                loc_acc[pl.ds(j * lanes + i * HEAD_DIM, HEAD_DIM), :] = blend

            @pl.when(s == 0)
            def _():
                st_buf[0, j] = loc_st[j]
                acc_buf[0, rows(j), :] = loc_acc[rows(j), :].astype(jnp.bfloat16)

            @pl.when(s > 0)
            def _():
                for copy in acc_copies(j, s - 1):
                    copy.wait_recv()
                for h in range(heads):
                    at, peak, total, blend = merged(j, s, h)
                    st_buf[s, j, h : h + 1, :] = peak
                    st_buf[s, j, heads + h : heads + h + 1, :] = total
                    acc_buf[s, at, :] = blend.astype(jnp.bfloat16)

            for copy in acc_copies(j, s):
                copy.start()
        return carry

    lax.fori_loop(0, n, step, 0)

    limit = span_ref[me]
    key_at = lax.broadcasted_iota(jnp.int32, (slots, slots), 0)
    slot_at = lax.broadcasted_iota(jnp.int32, (slots, slots), 1)
    allowed = (key_at <= slot_at) & (key_at < limit)
    for j in range(streams):
        for g in range(lanes // PAIR):
            base = j * lanes + g * PAIR
            k_pair = fk_ref[:, base : base + PAIR]
            v_t = fv_ref[:, base : base + PAIR].T
            q_pair = q_ref[base : base + PAIR, :]
            for h in range(2):
                scores = jnp.dot(
                    k_pair * keep[h], masked_query(q_pair, h), preferred_element_type=jnp.float32
                )
                scores = jnp.where(allowed, scores, NEG)
                peak, total, blend = attend(scores, v_t[h * HEAD_DIM : (h + 1) * HEAD_DIM])
                i = 2 * g + h
                loc_st[j, i : i + 1, :] = peak
                loc_st[j, heads + i : heads + i + 1, :] = total
                loc_acc[pl.ds(j * lanes + i * HEAD_DIM, HEAD_DIM), :] = blend
    for j in range(streams):
        for copy in acc_copies(j, n - 1):
            copy.wait_recv()
        for h in range(heads):
            at, _, total, blend = merged(j, n, h)
            out_ref[at, :] = (blend / total).astype(jnp.bfloat16)

    def drain(s, carry):
        for j in range(streams):

            @pl.when(s + 1 < n)
            def _():
                q_copy(j, s).wait_send()

            for copy in acc_copies(j, s):
                copy.wait_send()
        return carry

    lax.fori_loop(0, n, drain, 0)


def ring_attention(n, q_t, fresh_k, fresh_v, kv, cache_len, span_len):
    width, slots = q_t.shape
    keys = kv.shape[2]
    streams = 2 if width % (2 * PAIR) == 0 else 1
    lanes = width // streams
    stat_rows = -(-2 * (lanes // HEAD_DIM) // 8) * 8
    requests = kv.shape[1]
    vmem = pl.BlockSpec(memory_space=pltpu.VMEM)
    smem = pl.BlockSpec(memory_space=pltpu.SMEM)
    dma = pltpu.SemaphoreType.DMA
    return pl.pallas_call(
        functools.partial(ring_kernel, n, streams),
        out_shape=jax.ShapeDtypeStruct((width, slots), jnp.bfloat16),
        in_specs=[smem, smem, vmem, vmem, vmem, pl.BlockSpec(memory_space=pl.ANY)],
        out_specs=vmem,
        scratch_shapes=[
            pltpu.VMEM((n, width, slots), jnp.bfloat16),
            pltpu.VMEM((n + 1, width, slots), jnp.bfloat16),
            pltpu.VMEM((n + 1, streams, stat_rows, slots), jnp.float32),
            pltpu.VMEM((2, streams, 2, keys, lanes), jnp.bfloat16),
            pltpu.VMEM((2, keys, PAIR), jnp.bfloat16),
            pltpu.VMEM((width, slots), jnp.float32),
            pltpu.VMEM((streams, stat_rows, slots), jnp.float32),
            dma((streams, n)),
            dma((streams, n)),
            dma((streams, n)),
            dma((streams, n)),
            dma((streams, n)),
            dma((streams, n)),
            dma((2, streams)),
        ],
        compiler_params=pltpu.CompilerParams(
            collective_id=0, has_side_effects=True, vmem_limit_bytes=56 * 1024 * 1024
        ),
        cost_estimate=pl.CostEstimate(
            flops=4 * requests * width * slots * keys,
            bytes_accessed=2 * requests * keys * width * 2,
            transcendentals=requests * (width // HEAD_DIM) * slots * keys,
        ),
    )(cache_len, span_len, q_t, fresh_k, fresh_v, kv)


def shards(
    n,
    tp,
    tokens,
    w_qkv,
    w_out,
    w_up,
    b_up,
    w_down,
    b_down,
    ln1_gain,
    ln1_bias,
    ln2_gain,
    ln2_bias,
    kv_cache,
    cache_len,
    span_len,
):
    index = lax.axis_index("tp")
    half = tokens.shape[0]

    def f32_dot(a, b, dims):
        return lax.dot_general(a, b, (dims, ((), ())), preferred_element_type=jnp.float32)

    def ordered(own, other, axis):
        return jnp.where(
            index == 0,
            jnp.concatenate([own, other], axis=axis),
            jnp.concatenate([other, own], axis=axis),
        )

    def queries(rows):
        return f32_dot(w_qkv[:, 0], rows, ((0,), (1,))).astype(jnp.bfloat16) * jnp.bfloat16(
            HEAD_DIM**-0.5
        )

    def fresh(rows, which):
        return f32_dot(rows, w_qkv[:, which], ((1,), (0,))).astype(jnp.bfloat16)

    def feed_forward(rows):
        hidden = jax.nn.gelu(f32_dot(rows, w_up, ((1,), (0,))) + b_up, approximate=False)
        return f32_dot(hidden.astype(jnp.bfloat16), w_down, ((1,), (0,)))

    def first_norm(projected):
        return layer_norm(tokens.astype(jnp.float32) + projected, ln1_gain, ln1_bias).astype(
            jnp.bfloat16
        )

    if tp == 2:
        swap = functools.partial(lax.ppermute, axis_name="tp", perm=[(0, 1), (1, 0)])
        rows = ordered(tokens, swap(tokens), 0)
    else:
        rows = lax.all_gather(tokens, "tp", axis=0, tiled=True)
    attention = ring_attention(
        n, queries(rows), fresh(rows, 1), fresh(rows, 2), kv_cache, cache_len, span_len
    )
    if tp == 2:
        mine = lax.dynamic_slice_in_dim(attention, index * half, half, 1)
        theirs = lax.dynamic_slice_in_dim(attention, (1 - index) * half, half, 1)
        got = swap(f32_dot(theirs, w_out, ((0,), (0,))).astype(jnp.bfloat16))
        normed = first_norm(f32_dot(mine, w_out, ((0,), (0,))) + got.astype(jnp.float32))
        their_rows, summed = lax.optimization_barrier((swap(normed), feed_forward(normed)))
        part = half // 2
        back = [
            swap(feed_forward(their_rows[i * part : (i + 1) * part]).astype(jnp.bfloat16))
            for i in range(2)
        ]
        summed = summed + jnp.concatenate(back, axis=0).astype(jnp.float32)
    else:
        scatter = functools.partial(
            lax.psum_scatter, axis_name="tp", scatter_dimension=0, tiled=True
        )
        projected = scatter(f32_dot(attention, w_out, ((0,), (0,))).astype(jnp.bfloat16))
        normed = first_norm(projected.astype(jnp.float32))
        all_rows = lax.all_gather(normed, "tp", axis=0, tiled=True)
        summed = scatter(feed_forward(all_rows).astype(jnp.bfloat16)).astype(jnp.float32)
    return layer_norm(summed + b_down + normed.astype(jnp.float32), ln2_gain, ln2_bias).astype(
        jnp.bfloat16
    )


def solution(mesh):
    placed = (
        P(("req", "tp"), None),
        P(None, None, "tp"),
        P("tp", None),
        P(None, "tp"),
        P("tp"),
        P("tp", None),
        P(),
        P(),
        P(),
        P(),
        P(),
        P(None, None, "req", "tp"),
        P(),
        P(),
    )
    return jax.shard_map(
        functools.partial(shards, mesh.shape["req"], mesh.shape["tp"]),
        mesh=mesh,
        in_specs=placed,
        out_specs=P(("req", "tp"), None),
        check_vma=False,
    )
```
